32 devices in a mesh: grp: 4 (over z), seq: 8 (over y, x, core).
Axes of the slice: x: 2, y: 2, z: 4, core: 2. Of those that a mesh axis runs over, the one named last changes fastest.
Arguments:
- signal: bfloat16 [8192, 256], P(('grp', 'seq')), may hold values from -6 to 6
- cotangent: bfloat16 [8192, 256], P(('grp', 'seq')), may hold values from -6 to 6
- w_taps: bfloat16 [512, 1024], replicated, may hold values from -0.25 to 0.25
- gate_bias: float32 [1024], replicated, may hold values from -3 to 3
- w_out: bfloat16 [512, 256], replicated, may hold values from -0.25 to 0.25
Outputs:
- block_out: bfloat16 [8192, 256], P(('grp', 'seq'))
- grad_in: bfloat16 [8192, 256], P(('grp', 'seq'))
- grad_taps: float32 [512, 1024], P('seq')
- grad_bias: float32 [1024], P('seq')
- grad_out: float32 [512, 256], P('seq')
The draws below stay inside these ranges and needn't reach their ends.
All inputs are finite; a program needn't handle non-finite values.
Results may differ from the reference program's by a relative error of at most 0.0045.
Values may be sent and summed in bfloat16 or wider, within the bound.
A program may use at most 64 MiB of HBM per device.

```python
import jax
import jax.numpy as jnp
from jax import lax

CHANNEL_COUNT = 256
H = 512
TS = 256
DILATION_GAP = 512
TIME_STEPS = 8192


def block_levels(stream_key, dims, cuts, smallest, largest):
    factor_of, own = 1.0, jax.random.fold_in(stream_key, 6)
    for position, parts in cuts:
        steps = jnp.exp(jax.random.uniform(jax.random.fold_in(own, position), (parts,), jnp.float32, smallest / len(cuts), largest / len(cuts)))
        factor_of = factor_of * jnp.repeat(steps, dims[position] // parts).reshape([-1 if axis == position else 1 for axis in range(len(dims))])
    return factor_of


def normal_values(rng, extent, spread, bound, cuts=(), dtype=jnp.bfloat16):
    factor_of = block_levels(rng, extent, cuts, -0.22, 0.18) if cuts else 1.0
    entries = jax.random.normal(rng, extent, jnp.float32) * spread * factor_of
    return jnp.minimum(jnp.maximum(entries, -bound), bound).astype(dtype)


def setup_inputs(seed: int = 0) -> dict:
    streams_of = jax.random.split(jax.random.key(seed), 6)
    signal = normal_values(streams_of[0], (TIME_STEPS, CHANNEL_COUNT), 1.0, 6.0, ((0, 32),))
    cotangent = normal_values(streams_of[1], (TIME_STEPS, CHANNEL_COUNT), 1.0, 6.0, ((0, 32),))
    w_taps = normal_values(streams_of[2], (2 * CHANNEL_COUNT, 2 * H), (2 * CHANNEL_COUNT) ** -0.5, 0.25)
    gate_bias = normal_values(streams_of[3], (2 * H,), 0.5, 3.0, (), jnp.float32)
    w_out = normal_values(streams_of[4], (H, CHANNEL_COUNT), H ** -0.5, 0.25)
    return dict(signal=signal, cotangent=cotangent, w_taps=w_taps, gate_bias=gate_bias, w_out=w_out)


def reduced_row_axes(left, right):
    return lax.dot_general(left, right, (((0,), (0,)), ((), ())), preferred_element_type=jnp.float32)


def contract_cols(left, right):
    return lax.dot_general(left, right, (((1,), (1,)), ((), ())), preferred_element_type=jnp.float32)


def reference(signal, cotangent, w_taps, gate_bias, w_out):
    span = TS * 8
    blocks = TIME_STEPS // span
    lagged_input = jnp.concatenate([jnp.zeros((DILATION_GAP, CHANNEL_COUNT), jnp.bfloat16), signal[:TIME_STEPS - DILATION_GAP]], axis=0)

    def step(carry, items):
        grad_taps, grad_bias, grad_out = carry
        rows, delay_rows, cot_rows = items
        inputs = jnp.concatenate([delay_rows, rows], axis=1)
        preact = jnp.dot(inputs, w_taps, preferred_element_type=jnp.float32) + gate_bias
        squashed = jnp.tanh(preact[:, :H])
        opened = jax.nn.sigmoid(preact[:, H:])
        hidden_state = (squashed * opened).astype(jnp.bfloat16)
        output = (rows.astype(jnp.float32) + jnp.dot(hidden_state, w_out, preferred_element_type=jnp.float32)).astype(jnp.bfloat16)
        grad_hidden = contract_cols(cot_rows, w_out)
        grad_pre = jnp.concatenate([grad_hidden * opened * (1.0 - squashed * squashed),
                                    grad_hidden * squashed * opened * (1.0 - opened)], axis=1).astype(jnp.bfloat16)
        grad_out = grad_out + reduced_row_axes(hidden_state, cot_rows)
        grad_taps = grad_taps + reduced_row_axes(inputs, grad_pre)
        grad_bias = grad_bias + jnp.sum(grad_pre.astype(jnp.float32), axis=0)
        back = contract_cols(grad_pre, w_taps)
        nearby = cot_rows.astype(jnp.float32) + back[:, CHANNEL_COUNT:]
        return (grad_taps, grad_bias, grad_out), (output, nearby, back[:, :CHANNEL_COUNT])

    init = (jnp.zeros((2 * CHANNEL_COUNT, 2 * H), jnp.float32), jnp.zeros((2 * H,), jnp.float32), jnp.zeros((H, CHANNEL_COUNT), jnp.float32))
    items = (signal.reshape(blocks, span, CHANNEL_COUNT), lagged_input.reshape(blocks, span, CHANNEL_COUNT), cotangent.reshape(blocks, span, CHANNEL_COUNT))
    sums, outs = lax.scan(step, init, items)
    grad_taps, grad_bias, grad_out = sums
    block_out = outs[0].reshape(TIME_STEPS, CHANNEL_COUNT)
    nearby = outs[1].reshape(TIME_STEPS, CHANNEL_COUNT)
    tapped_signal = outs[2].reshape(TIME_STEPS, CHANNEL_COUNT)
    future_part = jnp.concatenate([tapped_signal[DILATION_GAP:], jnp.zeros((DILATION_GAP, CHANNEL_COUNT), jnp.float32)], axis=0)
    grad_in = (nearby + future_part).astype(jnp.bfloat16)
    return (block_out, grad_in, grad_taps, grad_bias, grad_out)
```

```python
import functools

import jax
import jax.numpy as jnp
from jax import lax
from jax.experimental import pallas as pl
from jax.experimental.pallas import tpu as pltpu
from jax.sharding import PartitionSpec as P

MESH = pl.DeviceIdType.MESH
F32 = jnp.float32
BF16 = jnp.bfloat16
UNIT_BLOCK = 256
LAG = 2


def dot(left, right, dims=((1,), (0,))):
    return lax.dot_general(left, right, (dims, ((), ())), preferred_element_type=F32)


def kernel(cfg, sig_ref, cot_ref, wt_ref, bias_ref, wo_ref, block_ref, gin_ref, taps_ref, gb_ref, gout_ref, *scratch):
    S, G, C, R, widths, split, bias_inside = cfg
    NP = len(widths)
    it = iter(scratch)
    take = lambda: next(it)
    lag, pre, gh, gp, hid, tap_s, tap_r = [take() for _ in range(7)]
    part = [take() for _ in range(NP)]
    core_r = [take() for _ in range(NP)]
    xs = [take() for _ in range(NP)]
    xr = [take() for _ in range(NP)]
    tot = [take() for _ in range(NP)]
    zs = [take() for _ in range(NP)]
    zr = [take() for _ in range(NP)]
    ag = [take() for _ in range(NP)]
    b0, b_core, b1, b_x, b2, b_z = [take() for _ in range(6)]
    halo_ss, halo_rs, core_ss, core_rs, x_ss, x_rs, z_ss, z_rs, a_ss, a_rs = [take() for _ in range(10)]
    BP = NP

    width = sig_ref.shape[1]
    units = wo_ref.shape[0]
    U = UNIT_BLOCK
    NB = units // U

    g = lax.axis_index("grp")
    s = lax.axis_index("seq")
    c = lax.rem(s, 2)
    q = s // 2
    flat = g * S + s
    has_prev = flat >= LAG
    has_next = flat < S * G - LAG
    nxt = lax.rem(flat + LAG, S * G)
    prv = lax.rem(flat + S * G - LAG, S * G)
    nxt_id = (nxt // S, lax.rem(nxt, S))
    prv_id = (prv // S, lax.rem(prv, S))
    other = (g, 2 * q + 1 - c)
    x_to = [(g, 2 * lax.rem(q + k, C) + c) for k in range(1, C)]
    z_to = [(lax.rem(g + k, G), s) for k in range(1, G)]

    barrier = pltpu.get_barrier_semaphore()
    for dev in [nxt_id, prv_id, other] + x_to + z_to:
        pl.semaphore_signal(barrier, inc=1, device_id=dev, device_id_type=MESH)
    pl.semaphore_wait(barrier, 3 + (C - 1) + (G - 1))

    def remote(src, dst, ss, rs, dev):
        return pltpu.make_async_remote_copy(
            src_ref=src, dst_ref=dst, send_sem=ss, recv_sem=rs, device_id=dev, device_id_type=MESH
        )

    halo = remote(sig_ref, lag, halo_ss.at[0], halo_rs.at[0], nxt_id)
    back = remote(tap_s, tap_r, halo_ss.at[1], halo_rs.at[1], prv_id)

    @pl.when(has_next)
    def _():
        halo.start()

    sig = sig_ref[...]
    pre[...] = dot(sig, wt_ref[width:, :]) + bias_ref[...]
    gh[...] = dot(cot_ref[...], wo_ref[...], ((1,), (1,)))

    @pl.when(has_prev)
    def _():
        halo.wait_recv()

    @pl.when(jnp.logical_not(has_prev))
    def _():
        lag[...] = jnp.zeros_like(lag)

    def core_copy(p):
        if p == BP:
            return remote(b0, b_core, core_ss.at[p], core_rs.at[p], other)
        return remote(part[p].at[1 - c], core_r[p], core_ss.at[p], core_rs.at[p], other)

    def x_copies(p):
        src, dst = (b1, b_x) if p == BP else (xs[p], xr[p])
        return [
            remote(
                src if p == BP else src.at[k],
                dst.at[k],
                x_ss.at[p, k],
                x_rs.at[p, k],
                x_to[k],
            )
            for k in range(C - 1)
        ]

    def z_copies(p):
        out = []
        for k in range(G - 1):
            to = lax.rem(g + k + 1, G)
            if p == BP:
                src, dst = b2, b_z.at[g]
            elif split:
                src, dst = zs[p].at[to], zr[p].at[k]
            else:
                src, dst = zs[p], zr[p].at[g]
            out.append(remote(src, dst, z_ss.at[p, k], z_rs.at[p, k], z_to[k]))
        return out

    def z_wait_recv(p):
        for k in range(G - 1):
            frm = lax.rem(g + G - k - 1, G)
            if p == BP:
                src, dst = b2, b_z.at[frm]
            elif split:
                src, dst = zs[p].at[frm], zr[p].at[k]
            else:
                src, dst = zs[p], zr[p].at[frm]
            remote(src, dst, z_ss.at[p, k], z_rs.at[p, k], z_to[k]).wait_recv()

    def a_copies(p):
        return [
            remote(ag[p].at[g], ag[p].at[g], a_ss.at[p, k], a_rs.at[p, k], z_to[k])
            for k in range(G - 1)
        ]

    def store_part(p, acc, base):
        for j in range(acc.shape[0] // R):
            n = base // R + j
            part[p][n % 2, n // 2] = acc[j * R : (j + 1) * R]

    def put(p, value):
        if p == NP - 1:
            gout_ref[...] = value
        else:
            taps_ref[:, p * U : (p + 1) * U] = value[:, :U]
            taps_ref[:, units + p * U : units + (p + 1) * U] = value[:, U:]

    def stage0(p):
        if p < NB:
            f_cols = slice(p * U, (p + 1) * U)
            g_cols = slice(units + p * U, units + (p + 1) * U)
            lagged = lag[...]
            filt = pre[:, f_cols] + dot(lagged, wt_ref[:width, f_cols])
            gate = pre[:, g_cols] + dot(lagged, wt_ref[:width, g_cols])
            t = jnp.tanh(filt)
            o = 0.5 * jnp.tanh(0.5 * gate) + 0.5
            hid[:, f_cols] = (t * o).astype(BF16)
            go = gh[:, f_cols] * o
            gp[:, f_cols] = (go * (1.0 - t * t)).astype(BF16)
            gp[:, g_cols] = (go * t * (1.0 - o)).astype(BF16)
            both = jnp.concatenate([gp[:, f_cols], gp[:, g_cols]], axis=1)
            store_part(p, dot(lagged, both, ((0,), (0,))), 0)
            store_part(p, dot(sig_ref[...], both, ((0,), (0,))), width)
        elif p == NB:
            store_part(p, dot(hid[...], cot_ref[...], ((0,), (0,))), 0)
        else:
            ones = jnp.ones((8, gp.shape[0]), BF16)
            b0[...] = dot(ones, gp[...])[0:1]
        core_copy(p).start()

    def stage1(p):
        core_copy(p).wait_recv()
        if p == BP:
            b1[...] = b0[...] + b_core[...]
        else:
            for k in range(C - 1):
                chip = lax.rem(q + k + 1, C)
                xs[p][k] = (part[p][c, chip] + core_r[p][chip]).astype(BF16)
        for copy in x_copies(p):
            copy.start()

    def stage2(p):
        for copy in x_copies(p):
            copy.wait_recv()
        if p == BP:
            total = b1[...]
            for k in range(C - 1):
                total = total + b_x[k]
            b2[...] = total
            b_z[g] = total
        else:
            total = part[p][c, q] + core_r[p][q]
            for k in range(C - 1):
                total = total + xr[p][k].astype(F32)
            if split:
                rows = R // G
                for j in range(G):
                    tot[p][j] = total[j * rows : (j + 1) * rows]
                    zs[p][j] = total[j * rows : (j + 1) * rows].astype(BF16)
            else:
                zs[p][...] = total.astype(BF16)
                zr[p][g] = total.astype(BF16)
        for copy in z_copies(p):
            copy.start()

    def stage3(p):
        z_wait_recv(p)
        if p == BP:
            total = b_z[0]
            for k in range(1, G):
                total = total + b_z[k]
            if bias_inside:
                share = gb_ref.shape[1]
                mine = total[:, :share]
                for j in range(1, S):
                    mine = jnp.where(s == j, total[:, j * share : (j + 1) * share], mine)
                gb_ref[...] = mine
            else:
                gb_ref[...] = total
        elif split:
            total = tot[p][g]
            for k in range(G - 1):
                total = total + zr[p][k].astype(F32)
            ag[p][g] = total.astype(BF16)
            for copy in a_copies(p):
                copy.start()
        else:
            total = zr[p][0].astype(F32)
            for k in range(1, G):
                total = total + zr[p][k].astype(F32)
            put(p, total)

    def stage4(p):
        if p == BP or not split:
            return
        for k in range(G - 1):
            frm = lax.rem(g + G - k - 1, G)
            remote(ag[p].at[g], ag[p].at[frm], a_ss.at[p, k], a_rs.at[p, k], z_to[k]).wait_recv()
        value = jnp.concatenate([ag[p][j].astype(F32) for j in range(G)], axis=0)
        put(p, value)

    for p in range(NB):
        stage0(p)
        if p > 0:
            stage1(p - 1)

    tap_s[...] = dot(gp[...], wt_ref[:width, :], ((1,), (1,))).astype(BF16)

    @pl.when(has_prev)
    def _():
        back.start()

    stage0(NB)
    stage1(NB - 1)
    stage0(BP)
    stage1(NB)
    stage1(BP)

    block_ref[...] = (sig_ref[...].astype(F32) + dot(hid[...], wo_ref[...])).astype(BF16)
    nearby = cot_ref[...].astype(F32) + dot(gp[...], wt_ref[width:, :], ((1,), (1,)))

    @pl.when(has_next)
    def _():
        back.wait_recv()

    @pl.when(jnp.logical_not(has_next))
    def _():
        tap_r[...] = jnp.zeros_like(tap_r)

    gin_ref[...] = (nearby + tap_r[...].astype(F32)).astype(BF16)

    for p in range(NP + 1 + 2):
        if p <= BP:
            stage2(p)
        if 0 <= p - 1 <= BP:
            stage3(p - 1)
        if 0 <= p - 2 <= BP:
            stage4(p - 2)

    @pl.when(has_next)
    def _():
        halo.wait_send()

    @pl.when(has_prev)
    def _():
        back.wait_send()

    for p in range(NP + 1):
        core_copy(p).wait_send()
        for copy in x_copies(p):
            copy.wait_send()
        for copy in z_copies(p):
            copy.wait_send()
        if p < NP and split:
            for copy in a_copies(p):
                copy.wait_send()


def per_device(S, G, signal, cotangent, w_taps, gate_bias, w_out):
    steps, width = signal.shape
    units = w_out.shape[0]
    C = S // 2
    R = 2 * width // S
    U = UNIT_BLOCK
    NB = units // U
    widths = [2 * U] * NB + [width]
    NP = len(widths)
    split = R % (16 * G) == 0
    share = 2 * units // S
    bias_inside = share % 128 == 0
    zrows = R // G if split else R
    V = pltpu.VMEM
    D = pltpu.SemaphoreType.DMA
    scratch = [
        V((steps, width), BF16),
        V((steps, 2 * units), F32),
        V((steps, units), F32),
        V((steps, 2 * units), BF16),
        V((steps, units), BF16),
        V((steps, width), BF16),
        V((steps, width), BF16),
    ]
    scratch += [V((2, C, R, w), F32) for w in widths]
    scratch += [V((C, R, w), F32) for w in widths]
    scratch += [V((C - 1, R, w), BF16) for w in widths]
    scratch += [V((C - 1, R, w), BF16) for w in widths]
    scratch += [V((G, zrows, w) if split else (8, 128), F32) for w in widths]
    scratch += [V((G, zrows, w) if split else (zrows, w), BF16) for w in widths]
    scratch += [V((G - 1 if split else G, zrows, w), BF16) for w in widths]
    scratch += [V((G, zrows, w) if split else (16, 128), BF16) for w in widths]
    one = (1, 2 * units)
    scratch += [V(one, F32), V(one, F32), V(one, F32), V((C - 1,) + one, F32), V(one, F32), V((G,) + one, F32)]
    scratch += [
        D((2,)), D((2,)),
        D((NP + 1,)), D((NP + 1,)),
        D((NP + 1, C - 1)), D((NP + 1, C - 1)),
        D((NP + 1, G - 1)), D((NP + 1, G - 1)),
        D((NP, G - 1)), D((NP, G - 1)),
    ]
    vmem = pl.BlockSpec(memory_space=pltpu.VMEM)
    outs = pl.pallas_call(
        functools.partial(kernel, (S, G, C, R, tuple(widths), split, bias_inside)),
        out_shape=(
            jax.ShapeDtypeStruct((steps, width), BF16),
            jax.ShapeDtypeStruct((steps, width), BF16),
            jax.ShapeDtypeStruct((R, 2 * units), F32),
            jax.ShapeDtypeStruct((1, share if bias_inside else 2 * units), F32),
            jax.ShapeDtypeStruct((units // S, width), F32),
        ),
        in_specs=[vmem] * 5,
        out_specs=[vmem] * 5,
        scratch_shapes=scratch,
        compiler_params=pltpu.CompilerParams(
            collective_id=0, has_side_effects=True, vmem_limit_bytes=48 * 1024 * 1024
        ),
        cost_estimate=pl.CostEstimate(
            flops=2 * steps * width * units * 16, bytes_accessed=4 << 20, transcendentals=2 * steps * units
        ),
    )(signal, cotangent, w_taps, gate_bias.reshape(1, -1), w_out)
    block_out, grad_in, grad_taps, grad_bias, grad_out = outs
    grad_bias = grad_bias.reshape(-1)
    if not bias_inside:
        grad_bias = lax.dynamic_slice_in_dim(grad_bias, lax.axis_index("seq") * share, share, 0)
    return block_out, grad_in, grad_taps, grad_bias, grad_out


def solution(mesh):
    S, G = mesh.shape["seq"], mesh.shape["grp"]
    rows = P(("grp", "seq"), None)
    return jax.shard_map(
        functools.partial(per_device, S, G),
        mesh=mesh,
        in_specs=(rows, rows, P(), P(), P()),
        out_specs=(rows, rows, P("seq", None), P("seq"), P("seq", None)),
        check_vma=False,
    )
```

```python
import functools

import jax
import jax.numpy as jnp
from jax import lax
from jax.experimental import pallas as pl
from jax.experimental.pallas import tpu as pltpu
from jax.sharding import PartitionSpec as P

MESH = pl.DeviceIdType.MESH
F32 = jnp.float32
BF16 = jnp.bfloat16
UNIT_BLOCK = 256
LAG = 2


def dot(left, right, dims=((1,), (0,))):
    return lax.dot_general(left, right, (dims, ((), ())), preferred_element_type=F32)


def kernel(cfg, sig_in, cot_in, wt_in, bias_in, wo_in, *rest):
    results, scratch = rest[:5], rest[5:]
    S, G, C, R, widths, split, bias_inside = cfg
    NP = len(widths)
    it = iter(scratch)
    take = lambda: next(it)
    sig_ref, cot_ref, wt_ref, bias_ref, wo_ref, in_sem = [take() for _ in range(6)]
    block_ref, gin_ref, taps_ref, gb_ref, gout_ref, out_sem, near = [take() for _ in range(7)]
    lag, pre, gh, gp, hid, tap_s, tap_r = [take() for _ in range(7)]
    part = [take() for _ in range(NP)]
    core_r = [take() for _ in range(NP)]
    xs = [take() for _ in range(NP)]
    xr = [take() for _ in range(NP)]
    tot = [take() for _ in range(NP)]
    zs = [take() for _ in range(NP)]
    zr = [take() for _ in range(NP)]
    ag = [take() for _ in range(NP)]
    b0, b_core, b1, b_x, b2, b_z = [take() for _ in range(6)]
    halo_ss, halo_rs, core_ss, core_rs, x_ss, x_rs, z_ss, z_rs, a_ss, a_rs = [take() for _ in range(10)]
    BP = NP

    width = sig_ref.shape[1]
    units = wo_ref.shape[0]
    U = UNIT_BLOCK
    NB = units // U

    g = lax.axis_index("grp")
    s = lax.axis_index("seq")
    c = lax.rem(s, 2)
    q = s // 2
    flat = g * S + s
    has_prev = flat >= LAG
    has_next = flat < S * G - LAG
    nxt = lax.rem(flat + LAG, S * G)
    prv = lax.rem(flat + S * G - LAG, S * G)
    nxt_id = (nxt // S, lax.rem(nxt, S))
    prv_id = (prv // S, lax.rem(prv, S))
    other = (g, 2 * q + 1 - c)
    x_to = [(g, 2 * lax.rem(q + k, C) + c) for k in range(1, C)]
    z_to = [(lax.rem(g + k, G), s) for k in range(1, G)]

    loads = [
        pltpu.make_async_copy(src, dst, in_sem.at[k])
        for k, (src, dst) in enumerate(
            [(sig_in, sig_ref), (wt_in, wt_ref), (bias_in, bias_ref), (cot_in, cot_ref), (wo_in, wo_ref)]
        )
    ]
    for load in loads:
        load.start()
    barrier = pltpu.get_barrier_semaphore()
    for dev in [nxt_id, prv_id, other] + x_to + z_to:
        pl.semaphore_signal(barrier, inc=1, device_id=dev, device_id_type=MESH)
    pl.semaphore_wait(barrier, 3 + (C - 1) + (G - 1))

    def remote(src, dst, ss, rs, dev):
        return pltpu.make_async_remote_copy(
            src_ref=src, dst_ref=dst, send_sem=ss, recv_sem=rs, device_id=dev, device_id_type=MESH
        )

    halo = remote(sig_in, lag, halo_ss.at[0], halo_rs.at[0], nxt_id)
    back = remote(tap_s, tap_r, halo_ss.at[1], halo_rs.at[1], prv_id)

    @pl.when(has_next)
    def _():
        halo.start()

    for load in loads[:3]:
        load.wait()
    pre[...] = dot(sig_ref[...], wt_ref[width:, :]) + bias_ref[...]
    for load in loads[3:]:
        load.wait()
    gh[...] = dot(cot_ref[...], wo_ref[...], ((1,), (1,)))

    @pl.when(has_prev)
    def _():
        halo.wait_recv()

    @pl.when(jnp.logical_not(has_prev))
    def _():
        lag[...] = jnp.zeros_like(lag)

    def core_copy(p):
        if p == BP:
            return remote(b0, b_core, core_ss.at[p], core_rs.at[p], other)
        return remote(part[p].at[1 - c], core_r[p], core_ss.at[p], core_rs.at[p], other)

    def x_copies(p):
        src, dst = (b1, b_x) if p == BP else (xs[p], xr[p])
        return [
            remote(
                src if p == BP else src.at[k],
                dst.at[k],
                x_ss.at[p, k],
                x_rs.at[p, k],
                x_to[k],
            )
            for k in range(C - 1)
        ]

    def z_copies(p):
        out = []
        for k in range(G - 1):
            to = lax.rem(g + k + 1, G)
            if p == BP:
                src, dst = b2, b_z.at[g]
            elif split:
                src, dst = zs[p].at[to], zr[p].at[k]
            else:
                src, dst = zs[p], zr[p].at[g]
            out.append(remote(src, dst, z_ss.at[p, k], z_rs.at[p, k], z_to[k]))
        return out

    def z_wait_recv(p):
        for k in range(G - 1):
            frm = lax.rem(g + G - k - 1, G)
            if p == BP:
                src, dst = b2, b_z.at[frm]
            elif split:
                src, dst = zs[p].at[frm], zr[p].at[k]
            else:
                src, dst = zs[p], zr[p].at[frm]
            remote(src, dst, z_ss.at[p, k], z_rs.at[p, k], z_to[k]).wait_recv()

    def a_copies(p):
        return [
            remote(ag[p].at[g], ag[p].at[g], a_ss.at[p, k], a_rs.at[p, k], z_to[k])
            for k in range(G - 1)
        ]

    def store_part(p, acc, base):
        for j in range(acc.shape[0] // R):
            n = base // R + j
            part[p][n % 2, n // 2] = acc[j * R : (j + 1) * R]

    def put(p, value):
        if p == NP - 1:
            gout_ref[...] = value
        else:
            taps_ref[:, p * U : (p + 1) * U] = value[:, :U]
            taps_ref[:, units + p * U : units + (p + 1) * U] = value[:, U:]

    def stage0(p):
        if p < NB:
            f_cols = slice(p * U, (p + 1) * U)
            g_cols = slice(units + p * U, units + (p + 1) * U)
            lagged = lag[...]
            filt = pre[:, f_cols] + dot(lagged, wt_ref[:width, f_cols])
            gate = pre[:, g_cols] + dot(lagged, wt_ref[:width, g_cols])
            t = jnp.tanh(filt)
            o = 0.5 * jnp.tanh(0.5 * gate) + 0.5
            hid[:, f_cols] = (t * o).astype(BF16)
            go = gh[:, f_cols] * o
            gp[:, f_cols] = (go * (1.0 - t * t)).astype(BF16)
            gp[:, g_cols] = (go * t * (1.0 - o)).astype(BF16)
            both = jnp.concatenate([gp[:, f_cols], gp[:, g_cols]], axis=1)
            store_part(p, dot(lagged, both, ((0,), (0,))), 0)
            store_part(p, dot(sig_ref[...], both, ((0,), (0,))), width)
        elif p == NB:
            store_part(p, dot(hid[...], cot_ref[...], ((0,), (0,))), 0)
        else:
            ones = jnp.ones((8, gp.shape[0]), BF16)
            b0[...] = dot(ones, gp[...])[0:1]
        core_copy(p).start()

    def stage1(p):
        core_copy(p).wait_recv()
        if p == BP:
            b1[...] = b0[...] + b_core[...]
        else:
            for k in range(C - 1):
                chip = lax.rem(q + k + 1, C)
                xs[p][k] = (part[p][c, chip] + core_r[p][chip]).astype(BF16)
        for copy in x_copies(p):
            copy.start()

    def stage2(p):
        for copy in x_copies(p):
            copy.wait_recv()
        if p == BP:
            total = b1[...]
            for k in range(C - 1):
                total = total + b_x[k]
            b2[...] = total
            b_z[g] = total
        else:
            total = part[p][c, q] + core_r[p][q]
            for k in range(C - 1):
                total = total + xr[p][k].astype(F32)
            if split:
                rows = R // G
                for j in range(G):
                    tot[p][j] = total[j * rows : (j + 1) * rows]
                    zs[p][j] = total[j * rows : (j + 1) * rows].astype(BF16)
            else:
                zs[p][...] = total.astype(BF16)
                zr[p][g] = total.astype(BF16)
        for copy in z_copies(p):
            copy.start()

    def stage3(p):
        z_wait_recv(p)
        if p == BP:
            total = b_z[0]
            for k in range(1, G):
                total = total + b_z[k]
            if bias_inside:
                share = gb_ref.shape[1]
                mine = total[:, :share]
                for j in range(1, S):
                    mine = jnp.where(s == j, total[:, j * share : (j + 1) * share], mine)
                gb_ref[...] = mine
            else:
                gb_ref[...] = total
        elif split:
            total = tot[p][g]
            for k in range(G - 1):
                total = total + zr[p][k].astype(F32)
            ag[p][g] = total.astype(BF16)
            for copy in a_copies(p):
                copy.start()
        else:
            total = zr[p][0].astype(F32)
            for k in range(1, G):
                total = total + zr[p][k].astype(F32)
            put(p, total)

    def stage4(p):
        if p == BP or not split:
            return
        for k in range(G - 1):
            frm = lax.rem(g + G - k - 1, G)
            remote(ag[p].at[g], ag[p].at[frm], a_ss.at[p, k], a_rs.at[p, k], z_to[k]).wait_recv()
        value = jnp.concatenate([ag[p][j].astype(F32) for j in range(G)], axis=0)
        put(p, value)

    stores = [
        pltpu.make_async_copy(src, dst, out_sem.at[k])
        for k, (src, dst) in enumerate(zip((block_ref, gin_ref, taps_ref, gb_ref, gout_ref), results))
    ]

    def sent(p):
        for copy in x_copies(p):
            copy.wait_send()

    stage0(0)
    for p in range(1, NB):
        stage0(p)
    stage1(0)
    stage0(NB)
    stage0(BP)
    tap_s[...] = dot(gp[...], wt_ref[:width, :], ((1,), (1,))).astype(BF16)
    block_ref[...] = (sig_ref[...].astype(F32) + dot(hid[...], wo_ref[...])).astype(BF16)
    stores[0].start()
    near[...] = cot_ref[...].astype(F32) + dot(gp[...], wt_ref[width:, :], ((1,), (1,)))
    stage1(BP)
    for step in range(1, NP + 3):
        if step < NP:
            sent(step - 1)
            stage1(step)
        if step == NP:
            sent(NP - 1)

            @pl.when(has_prev)
            def _():
                back.start()

        if step == 2:
            stage2(BP)
        if step == 3:
            stage3(BP)
            stores[3].start()
        if step - 1 < NP:
            stage2(step - 1)
        if 0 <= step - 2 < NP:
            stage3(step - 2)
        if 0 <= step - 3 < NP:
            stage4(step - 3)
            if step - 3 == NB - 1:
                stores[2].start()

    @pl.when(has_next)
    def _():
        back.wait_recv()

    @pl.when(jnp.logical_not(has_next))
    def _():
        tap_r[...] = jnp.zeros_like(tap_r)

    gin_ref[...] = (near[...] + tap_r[...].astype(F32)).astype(BF16)
    stores[1].start()
    stores[4].start()

    @pl.when(has_next)
    def _():
        halo.wait_send()

    @pl.when(has_prev)
    def _():
        back.wait_send()

    for p in range(NP + 1):
        core_copy(p).wait_send()
        if p == BP:
            sent(p)
        for copy in z_copies(p):
            copy.wait_send()
        if p < NP and split:
            for copy in a_copies(p):
                copy.wait_send()
    for store in stores:
        store.wait()


def write_out(*refs):
    ins, outs, sem = refs[:5], refs[5:10], refs[10]
    copies = [pltpu.make_async_copy(ins[k], outs[k], sem.at[k]) for k in range(5)]
    for copy in copies:
        copy.start()
    for copy in copies:
        copy.wait()


def per_device(S, G, signal, cotangent, w_taps, gate_bias, w_out):
    steps, width = signal.shape
    units = w_out.shape[0]
    C = S // 2
    R = 2 * width // S
    U = UNIT_BLOCK
    NB = units // U
    widths = [2 * U] * NB + [width]
    NP = len(widths)
    split = R % (16 * G) == 0
    share = 2 * units // S
    bias_inside = share % 128 == 0
    zrows = R // G if split else R
    V = pltpu.VMEM
    D = pltpu.SemaphoreType.DMA
    scratch = [
        V((steps, width), BF16),
        V((steps, width), BF16),
        V((2 * width, 2 * units), BF16),
        V((1, 2 * units), F32),
        V((units, width), BF16),
        D((5,)),
        V((steps, width), BF16),
        V((steps, width), BF16),
        V((R, 2 * units), F32),
        V((1, share if bias_inside else 2 * units), F32),
        V((units // S, width), F32),
        D((5,)),
        V((steps, width), F32),
        V((steps, width), BF16),
        V((steps, 2 * units), F32),
        V((steps, units), F32),
        V((steps, 2 * units), BF16),
        V((steps, units), BF16),
        V((steps, width), BF16),
        V((steps, width), BF16),
    ]
    scratch += [V((2, C, R, w), F32) for w in widths]
    scratch += [V((C, R, w), F32) for w in widths]
    scratch += [V((C - 1, R, w), BF16) for w in widths]
    scratch += [V((C - 1, R, w), BF16) for w in widths]
    scratch += [V((G, zrows, w) if split else (8, 128), F32) for w in widths]
    scratch += [V((G, zrows, w) if split else (zrows, w), BF16) for w in widths]
    scratch += [V((G - 1 if split else G, zrows, w), BF16) for w in widths]
    scratch += [V((G, zrows, w) if split else (16, 128), BF16) for w in widths]
    one = (1, 2 * units)
    scratch += [V(one, F32), V(one, F32), V(one, F32), V((C - 1,) + one, F32), V(one, F32), V((G,) + one, F32)]
    scratch += [
        D((2,)), D((2,)),
        D((NP + 1,)), D((NP + 1,)),
        D((NP + 1, C - 1)), D((NP + 1, C - 1)),
        D((NP + 1, G - 1)), D((NP + 1, G - 1)),
        D((NP, G - 1)), D((NP, G - 1)),
    ]
    vmem = pl.BlockSpec(memory_space=pltpu.VMEM)
    outs = pl.pallas_call(
        functools.partial(kernel, (S, G, C, R, tuple(widths), split, bias_inside)),
        out_shape=(
            jax.ShapeDtypeStruct((steps, width), BF16),
            jax.ShapeDtypeStruct((steps, width), BF16),
            jax.ShapeDtypeStruct((R, 2 * units), F32),
            jax.ShapeDtypeStruct((1, share if bias_inside else 2 * units), F32),
            jax.ShapeDtypeStruct((units // S, width), F32),
        ),
        in_specs=[pl.BlockSpec(memory_space=pltpu.HBM)] * 5,
        out_specs=[pl.BlockSpec(memory_space=pltpu.HBM)] * 5,
        scratch_shapes=scratch,
        compiler_params=pltpu.CompilerParams(
            collective_id=0, has_side_effects=True, vmem_limit_bytes=64000 * 1024
        ),
        cost_estimate=pl.CostEstimate(
            flops=2 * steps * width * units * 16, bytes_accessed=4 << 20, transcendentals=2 * steps * units
        ),
    )(signal, cotangent, w_taps, gate_bias.reshape(1, -1), w_out)
    block_out, grad_in, grad_taps, grad_bias, grad_out = pl.pallas_call(
        write_out,
        out_shape=tuple(jax.ShapeDtypeStruct(o.shape, o.dtype) for o in outs),
        in_specs=[vmem] * 5,
        out_specs=[pl.BlockSpec(memory_space=pltpu.HBM)] * 5,
        scratch_shapes=[D((5,))],
    )(*outs)
    grad_bias = grad_bias.reshape(-1)
    if not bias_inside:
        grad_bias = lax.dynamic_slice_in_dim(grad_bias, lax.axis_index("seq") * share, share, 0)
    return block_out, grad_in, grad_taps, grad_bias, grad_out


def solution(mesh):
    S, G = mesh.shape["seq"], mesh.shape["grp"]
    rows = P(("grp", "seq"), None)
    return jax.shard_map(
        functools.partial(per_device, S, G),
        mesh=mesh,
        in_specs=(rows, rows, P(), P(), P()),
        out_specs=(rows, rows, P("seq", None), P("seq"), P("seq", None)),
        check_vma=False,
    )
```

```python
import functools

import jax
import jax.numpy as jnp
from jax import lax
from jax.experimental import pallas as pl
from jax.experimental.pallas import tpu as pltpu
from jax.sharding import PartitionSpec as P

MESH = pl.DeviceIdType.MESH
F32 = jnp.float32
BF16 = jnp.bfloat16
UNIT_BLOCK = 256
GROUPS = 3
LAYOUT = {(2, 3): ((0,), (1,), (2,)), (2, 2): ((0,), (1, 2)), (1, 2): ((0,), (1,)), (2, 1): ((0, 1, 2),), (1, 1): ((0, 1),)}
BIAS_LANES = 128
LAG = 2


def dot(left, right, dims=((1,), (0,))):
    return lax.dot_general(left, right, (dims, ((), ())), preferred_element_type=F32)


def kernel(cfg, sig_in, cot_in, wt_in, bias_in, wo_in, *rest):
    results, scratch = rest[:5], rest[5:]
    S, G, C, R, pieces, split = cfg
    NP = len(pieces)
    it = iter(scratch)
    take = lambda: next(it)
    sig_ref, cot_ref, wt_ref, bias_ref, wo_ref, in_sem = [take() for _ in range(6)]
    block_ref, gin_ref, taps_ref, gb_ref, gout_ref, out_sem, near = [take() for _ in range(7)]
    lag, pre, gh, gp, hid, tap_s, tap_r = [take() for _ in range(7)]
    part = [take() for _ in range(NP)]
    core_r = [take() for _ in range(NP)]
    xs = [take() for _ in range(NP)]
    xr = [take() for _ in range(NP)]
    tot = [take() for _ in range(NP)]
    zs = [take() for _ in range(NP)]
    zr = [take() for _ in range(NP)]
    ag = [take() for _ in range(NP)]
    halo_ss, halo_rs, core_ss, core_rs, x_ss, x_rs, z_ss, z_rs, a_ss, a_rs = [take() for _ in range(10)]

    width = sig_ref.shape[1]
    units = wo_ref.shape[0]
    U = UNIT_BLOCK
    NB = units // U

    g = lax.axis_index("grp")
    s = lax.axis_index("seq")
    c = lax.rem(s, 2)
    q = s // 2
    flat = g * S + s
    has_prev = flat >= LAG
    has_next = flat < S * G - LAG
    nxt = lax.rem(flat + LAG, S * G)
    prv = lax.rem(flat + S * G - LAG, S * G)
    nxt_id = (nxt // S, lax.rem(nxt, S))
    prv_id = (prv // S, lax.rem(prv, S))
    other = (g, 2 * q + 1 - c)
    x_to = [(g, 2 * lax.rem(q + k, C) + c) for k in range(1, C)]
    z_to = [(lax.rem(g + k, G), s) for k in range(1, G)]

    loads = [
        pltpu.make_async_copy(src, dst, in_sem.at[k])
        for k, (src, dst) in enumerate(
            [(sig_in, sig_ref), (wt_in, wt_ref), (bias_in, bias_ref), (cot_in, cot_ref), (wo_in, wo_ref)]
        )
    ]
    for load in loads:
        load.start()
    barrier = pltpu.get_barrier_semaphore()
    for dev in [nxt_id, prv_id, other] + x_to + z_to:
        pl.semaphore_signal(barrier, inc=1, device_id=dev, device_id_type=MESH)
    pl.semaphore_wait(barrier, 3 + (C - 1) + (G - 1))

    def remote(src, dst, ss, rs, dev):
        return pltpu.make_async_remote_copy(
            src_ref=src, dst_ref=dst, send_sem=ss, recv_sem=rs, device_id=dev, device_id_type=MESH
        )

    halo = remote(sig_in, lag, halo_ss.at[0], halo_rs.at[0], nxt_id)
    back = remote(tap_s, tap_r, halo_ss.at[1], halo_rs.at[1], prv_id)

    @pl.when(has_next)
    def _():
        halo.start()

    for load in loads[:3]:
        load.wait()
    pre[...] = dot(sig_ref[...], wt_ref[width:, :]) + bias_ref[...]
    for load in loads[3:]:
        load.wait()
    gh[...] = dot(cot_ref[...], wo_ref[...], ((1,), (1,)))

    @pl.when(has_prev)
    def _():
        halo.wait_recv()

    @pl.when(jnp.logical_not(has_prev))
    def _():
        lag[...] = jnp.zeros_like(lag)

    def core_copy(p):
        return remote(part[p].at[1 - c], core_r[p], core_ss.at[p], core_rs.at[p], other)

    def x_copies(p):
        return [
            remote(xs[p].at[k], xr[p].at[k], x_ss.at[p], x_rs.at[p], x_to[k])
            for k in range(C - 1)
        ]

    def x_all(p):
        return remote(xs[p], xr[p], x_ss.at[p], x_rs.at[p], other)

    def z_copies(p):
        out = []
        for k in range(G - 1):
            if split:
                src, dst = zs[p].at[lax.rem(g + k + 1, G)], zr[p].at[k]
            else:
                src, dst = zs[p], zr[p].at[k]
            out.append(remote(src, dst, z_ss.at[p], z_rs.at[p], z_to[k]))
        return out

    def z_all(p):
        return remote(zr[p], zr[p], z_ss.at[p], z_rs.at[p], other)

    def a_copies(p):
        return [
            remote(ag[p].at[g], ag[p].at[g], a_ss.at[p], a_rs.at[p], z_to[k]) for k in range(G - 1)
        ]

    def a_all(p):
        rest = ag[p].at[pl.ds(0, G - 1)]
        return remote(rest, rest, a_ss.at[p], a_rs.at[p], other)

    def store_part(p, col, acc, base):
        for j in range(acc.shape[0] // R):
            n = base // R + j
            part[p][n % 2, n // 2, :, col : col + acc.shape[1]] = acc[j * R : (j + 1) * R]

    def put(p, value):
        for block, col in pieces[p][0]:
            if block == NB:
                gout_ref[...] = value[:, col : col + width]
                share = gb_ref.shape[1]
                gb_ref[...] = value[0:1, col + width : col + width + share]
            else:
                taps_ref[:, block * U : (block + 1) * U] = value[:, col : col + U]
                taps_ref[:, units + block * U : units + (block + 1) * U] = value[:, col + U : col + 2 * U]

    def compute(p, block, col):
        if block < NB:
            b = block
            f_cols = slice(b * U, (b + 1) * U)
            g_cols = slice(units + b * U, units + (b + 1) * U)
            lagged = lag[...]
            filt = pre[:, f_cols] + dot(lagged, wt_ref[:width, f_cols])
            gate = pre[:, g_cols] + dot(lagged, wt_ref[:width, g_cols])
            t = jnp.tanh(filt)
            o = 0.5 * jnp.tanh(0.5 * gate) + 0.5
            hid[:, f_cols] = (t * o).astype(BF16)
            go = gh[:, f_cols] * o
            gp[:, f_cols] = (go * (1.0 - t * t)).astype(BF16)
            gp[:, g_cols] = (go * t * (1.0 - o)).astype(BF16)
            both = jnp.concatenate([gp[:, f_cols], gp[:, g_cols]], axis=1)
            store_part(p, col, dot(lagged, both, ((0,), (0,))), 0)
            store_part(p, col, dot(sig_ref[...], both, ((0,), (0,))), width)
        else:
            store_part(p, col, dot(hid[...], cot_ref[...], ((0,), (0,))), 0)
            ones = jnp.ones((8, gp.shape[0]), BF16)
            sums = dot(ones, gp[...])[0:1]
            part[p][:, :, :, col + width :] = jnp.zeros((2, C, R, BIAS_LANES), F32)
            share = gb_ref.shape[1]
            for n in range(S):
                part[p][n % 2, n // 2, 0:1, col + width : col + width + share] = sums[:, n * share : (n + 1) * share]

    def stage0(p):
        for block, col in pieces[p][0]:
            compute(p, block, col)
        core_copy(p).start()

    def stage1(p):
        core_copy(p).wait_recv()
        for k in range(C - 1):
            chip = lax.rem(q + k + 1, C)
            xs[p][k] = (part[p][c, chip] + core_r[p][chip]).astype(BF16)
        for copy in x_copies(p):
            copy.start()

    def stage2(p):
        total = part[p][c, q] + core_r[p][q]
        x_all(p).wait_recv()
        for k in range(C - 1):
            total = total + xr[p][k].astype(F32)
        if split:
            rows = R // G
            for j in range(G):
                tot[p][j] = total[j * rows : (j + 1) * rows]
                zs[p][j] = total[j * rows : (j + 1) * rows].astype(BF16)
        else:
            zs[p][...] = total.astype(BF16)
        for copy in z_copies(p):
            copy.start()

    def stage3(p):
        z_all(p).wait_recv()
        if split:
            total = tot[p][g]
            for k in range(G - 1):
                total = total + zr[p][k].astype(F32)
            ag[p][g] = total.astype(BF16)
            for copy in a_copies(p):
                copy.start()
        else:
            for k in range(G - 1):
                ag[p][lax.rem(g + G - k - 1, G)] = zr[p][k]
            ag[p][g] = zs[p][...]
            total = ag[p][0].astype(F32)
            for k in range(1, G):
                total = total + ag[p][k].astype(F32)
            put(p, total)

    def stage4(p):
        if not split:
            return
        a_all(p).wait_recv()
        put(p, jnp.concatenate([ag[p][j].astype(F32) for j in range(G)], axis=0))

    stores = [
        pltpu.make_async_copy(src, dst, out_sem.at[k])
        for k, (src, dst) in enumerate(zip((block_ref, gin_ref, taps_ref, gb_ref, gout_ref), results))
    ]

    def sent(p):
        x_all(p).wait_send()

    stage0(0)
    if NP > 1:
        stage0(1)
    stage1(0)
    for p in range(2, NP):
        stage0(p)
    tap_s[...] = dot(gp[...], wt_ref[:width, :], ((1,), (1,))).astype(BF16)
    block_ref[...] = (sig_ref[...].astype(F32) + dot(hid[...], wo_ref[...])).astype(BF16)
    stores[0].start()
    near[...] = cot_ref[...].astype(F32) + dot(gp[...], wt_ref[width:, :], ((1,), (1,)))
    for step in range(1, NP + 3):
        if step < NP:
            sent(step - 1)
            stage1(step)
        if step == NP:
            sent(NP - 1)

            @pl.when(has_prev)
            def _():
                back.start()

        if step - 1 < NP:
            stage2(step - 1)
        if 0 <= step - 2 < NP:
            stage3(step - 2)
        if 0 <= step - 3 < NP:
            stage4(step - 3)

    @pl.when(has_next)
    def _():
        back.wait_recv()

    @pl.when(jnp.logical_not(has_next))
    def _():
        tap_r[...] = jnp.zeros_like(tap_r)

    gin_ref[...] = (near[...] + tap_r[...].astype(F32)).astype(BF16)
    for store in stores[1:]:
        store.start()

    @pl.when(has_next)
    def _():
        halo.wait_send()

    @pl.when(has_prev)
    def _():
        back.wait_send()

    for p in range(NP):
        core_copy(p).wait_send()
        z_all(p).wait_send()
        if split:
            a_all(p).wait_send()
    for store in stores:
        store.wait()


def write_out(*refs):
    ins, outs, sem = refs[:5], refs[5:10], refs[10]
    copies = [pltpu.make_async_copy(ins[k], outs[k], sem.at[k]) for k in range(5)]
    for copy in copies:
        copy.start()
    for copy in copies:
        copy.wait()


def per_device(S, G, signal, cotangent, w_taps, gate_bias, w_out):
    steps, width = signal.shape
    units = w_out.shape[0]
    C = S // 2
    R = 2 * width // S
    U = UNIT_BLOCK
    NB = units // U
    sizes = [2 * U] * NB + [width + BIAS_LANES]
    pieces = []
    for members in LAYOUT[NB, GROUPS]:
        placed, at = [], 0
        for block in members:
            placed.append((block, at))
            at += sizes[block]
        pieces.append((tuple(placed), at))
    widths = [w for _, w in pieces]
    NP = len(pieces)
    split = R % (16 * G) == 0
    share = 2 * units // S
    zrows = R // G if split else R
    V = pltpu.VMEM
    D = pltpu.SemaphoreType.DMA
    scratch = [
        V((steps, width), BF16),
        V((steps, width), BF16),
        V((2 * width, 2 * units), BF16),
        V((1, 2 * units), F32),
        V((units, width), BF16),
        D((5,)),
        V((steps, width), BF16),
        V((steps, width), BF16),
        V((R, 2 * units), F32),
        V((1, share), F32),
        V((units // S, width), F32),
        D((5,)),
        V((steps, width), F32),
        V((steps, width), BF16),
        V((steps, 2 * units), F32),
        V((steps, units), F32),
        V((steps, 2 * units), BF16),
        V((steps, units), BF16),
        V((steps, width), BF16),
        V((steps, width), BF16),
    ]
    scratch += [V((2, C, R, w), F32) for w in widths]
    scratch += [V((C, R, w), F32) for w in widths]
    scratch += [V((C - 1, R, w), BF16) for w in widths]
    scratch += [V((C - 1, R, w), BF16) for w in widths]
    scratch += [V((G, zrows, w) if split else (8, 128), F32) for w in widths]
    scratch += [V((G, zrows, w) if split else (zrows, w), BF16) for w in widths]
    scratch += [V((G - 1, zrows, w), BF16) for w in widths]
    scratch += [V((G, zrows, w), BF16) for w in widths]
    scratch += [D((2,)), D((2,))] + [D((NP,)) for _ in range(8)]
    vmem = pl.BlockSpec(memory_space=pltpu.VMEM)
    outs = pl.pallas_call(
        functools.partial(kernel, (S, G, C, R, tuple(pieces), split)),
        out_shape=(
            jax.ShapeDtypeStruct((steps, width), BF16),
            jax.ShapeDtypeStruct((steps, width), BF16),
            jax.ShapeDtypeStruct((R, 2 * units), F32),
            jax.ShapeDtypeStruct((1, share), F32),
            jax.ShapeDtypeStruct((units // S, width), F32),
        ),
        in_specs=[pl.BlockSpec(memory_space=pltpu.HBM)] * 5,
        out_specs=[pl.BlockSpec(memory_space=pltpu.HBM)] * 5,
        scratch_shapes=scratch,
        compiler_params=pltpu.CompilerParams(
            collective_id=0, has_side_effects=True, vmem_limit_bytes=64000 * 1024
        ),
        cost_estimate=pl.CostEstimate(
            flops=2 * steps * width * units * 16, bytes_accessed=4 << 20, transcendentals=2 * steps * units
        ),
    )(signal, cotangent, w_taps, gate_bias.reshape(1, -1), w_out)
    block_out, grad_in, grad_taps, grad_bias, grad_out = pl.pallas_call(
        write_out,
        out_shape=tuple(jax.ShapeDtypeStruct(o.shape, o.dtype) for o in outs),
        in_specs=[vmem] * 5,
        out_specs=[pl.BlockSpec(memory_space=pltpu.HBM)] * 5,
        scratch_shapes=[D((5,))],
    )(*outs)
    grad_bias = grad_bias.reshape(-1)
    return block_out, grad_in, grad_taps, grad_bias, grad_out


def solution(mesh):
    S, G = mesh.shape["seq"], mesh.shape["grp"]
    rows = P(("grp", "seq"), None)
    return jax.shard_map(
        functools.partial(per_device, S, G),
        mesh=mesh,
        in_specs=(rows, rows, P(), P(), P()),
        out_specs=(rows, rows, P("seq", None), P("seq"), P("seq", None)),
        check_vma=False,
    )
```
